256 devices in a mesh: dp: 2 (over core), ctx: 32 (over x, z), tp: 4 (over y).
Axes of the slice: x: 4, y: 4, z: 8, core: 2. Of those that a mesh axis runs over, the one named last changes fastest.
Arguments:
- queries: bfloat16 [8192, 4096], P(('dp', 'ctx'), 'tp'), parts along dimension 0, may hold values from -8 to 8
- keys: bfloat16 [64, 1601, 512], P(('dp', 'ctx'), None, 'tp'), parts along dimension 0, may hold values from -6 to 6
- values: bfloat16 [64, 1601, 512], P(('dp', 'ctx'), None, 'tp'), parts along dimension 0, may hold values from -6 to 6
- refs: int32 [64, 4], P(('dp', 'ctx')), parts along dimension 0, may hold values from -1 to 31, as said below
- upstream: bfloat16 [8192, 4096], P(('dp', 'ctx'), 'tp'), parts along dimension 0, may hold values from -6 to 6
Outputs:
- attended: bfloat16 [8192, 4096], P(('dp', 'ctx'), 'tp'), parts along dimension 0
- query_grad: bfloat16 [8192, 4096], P(('dp', 'ctx'), 'tp'), parts along dimension 0
- key_grad: float32 [64, 1601, 512], P(('dp', 'ctx'), None, 'tp'), parts along dimension 0
- value_grad: float32 [64, 1601, 512], P(('dp', 'ctx'), None, 'tp'), parts along dimension 0
The draws below stay inside these ranges and needn't reach their ends.
There are 2 independent parts, one for each index of `dp`. The reference program is written for one: setup_inputs(seed, part) draws one part's arguments, and reference() takes and returns one part's arrays. A program takes and returns all parts, laid end to end along the dimension named above; each array names one. Nothing has to cross between parts.
Inputs may be any that keep to these rules, and one draw needn't show every extreme that they name: `refs`: row b lists the images that text block b attends: 1 to 4 distinct ids first, then -1 in the unused slots. Every id i satisfies (b - 3) <= i < (b + 1), so images are held in document order, 1 to each device of ctx. Block 0 names one image; the last block names 4, image 32 - 1 among them.
All inputs are finite; a program needn't handle non-finite values.
Results may differ from the reference program's by a relative error of at most 0.0081.
Values may be sent and summed in bfloat16 or wider, within the bound.
A program may use at most 64 MiB of HBM per device.

```python
import jax
import jax.numpy as jnp
from jax import lax

HEADS = 32
KVH = 4
HD = 128
IMG_TOK = 1601
BLOCK = 128
MAXREF = 4
REACH = 3
IMG_DEV = 1
BLK_DEV = 1
TOKENS = 4096
BLOCKS = 32
IMAGES = 32


def draw_queries(key, part):
    key = jax.random.fold_in(key, 1)
    shape = (TOKENS, HEADS, HD)
    drawn = jnp.clip(jax.random.normal(key, shape, jnp.float32), -6.0, 6.0)
    return drawn.reshape(TOKENS, HEADS * HD).astype(jnp.bfloat16)


def draw_keys(key, part):
    key = jax.random.fold_in(key, 2)
    shape = (IMAGES, IMG_TOK, KVH, HD)
    drawn = jnp.clip(jax.random.normal(key, shape, jnp.float32), -6.0, 6.0)
    return drawn.reshape(IMAGES, IMG_TOK, KVH * HD).astype(jnp.bfloat16)


def draw_refs(key, part):
    key = jax.random.fold_in(key, 5)
    first_key, second_key = jax.random.split(key)
    cand_count = (REACH + 1) * IMG_DEV
    block_pos = jnp.arange(BLOCKS, dtype=jnp.int32)
    lowest = (block_pos // BLK_DEV - REACH) * IMG_DEV
    orders = jax.vmap(lambda block_key: jax.random.permutation(block_key, cand_count))(jax.random.split(first_key, BLOCKS))
    cand_ids = lowest[:, None] + orders.astype(jnp.int32)
    valid = cand_ids >= 0
    ranking = jnp.where(valid, 0, cand_count) + jnp.arange(cand_count, dtype=jnp.int32)[None, :]
    top_first = (block_pos == BLOCKS - 1)[:, None] & (cand_ids == IMAGES - 1)
    ranking = ranking - jnp.where(top_first, 2 * cand_count, 0)
    picked = jnp.argsort(ranking, axis=1)[:, :MAXREF]
    chosen = jnp.take_along_axis(cand_ids, picked, axis=1)
    chosen_valid = jnp.take_along_axis(valid, picked, axis=1)
    count_table = jnp.minimum(jnp.array([1, 1, 1, 1, 1, 1, 1, 1, 2, 2, 2, 2, 3, 3, 4, 4], jnp.int32), MAXREF)
    counts = count_table[jax.random.randint(second_key, (BLOCKS,), 0, 16)]
    counts = jnp.where(block_pos == BLOCKS - 1, MAXREF, counts)
    counts = jnp.where(block_pos == 0, 1, counts)
    keep = (jnp.arange(MAXREF, dtype=jnp.int32)[None, :] < counts[:, None]) & chosen_valid
    return jnp.where(keep, chosen, -1).astype(jnp.int32)


def block_scale(own_key, shape, shards, least, largest):
    loudness = 1.0
    for position, parts in shards:
        draws = jax.random.uniform(jax.random.fold_in(jax.random.fold_in(own_key, 6), position), (parts,), jnp.float32, least / len(shards), largest / len(shards))
        loudness = loudness * jnp.repeat(jnp.exp(draws), shape[position] // parts).reshape((-1,) + (1,) * (len(shape) - 1 - position))
    return loudness


def gaussian(stream_key, shape, spread, limit, cuts=(), kind=jnp.bfloat16):
    gain = block_scale(stream_key, shape, cuts, -0.22, 0.18) if cuts else 1.0
    values = jax.random.normal(stream_key, shape, jnp.float32) * spread * gain
    return jnp.minimum(jnp.maximum(values, -limit), limit).astype(kind)


def setup_inputs(seed: int = 0, part: int = 0) -> dict:
    key_list = jax.random.split(jax.random.key(seed), 6)
    part_splits = jax.random.split(jax.random.fold_in(key_list[5], part), 6)
    queries = draw_queries(jax.random.fold_in(jax.random.fold_in(key_list[5], part), 71), part)
    keys = draw_keys(jax.random.fold_in(jax.random.fold_in(key_list[5], part), 71), part)
    values = gaussian(part_splits[2], (IMAGES, IMG_TOK, KVH * HD), 1.0, 6.0, ((0, 32), (2, 4)))
    refs = draw_refs(jax.random.fold_in(jax.random.fold_in(key_list[5], part), 71), part)
    upstream = gaussian(part_splits[4], (TOKENS, HEADS * HD), 1.0, 6.0, ((0, 32), (1, 4)))
    return {"queries": queries, "keys": keys, "values": values, "refs": refs, "upstream": upstream}


def reference(queries, keys, values, refs, upstream):
    score_scale = HD ** -0.5
    group_size = HEADS // KVH
    key_width = KVH * HD

    def block_terms(block_id):
        q_rows = lax.dynamic_slice_in_dim(queries, block_id * BLOCK, BLOCK, 0).astype(jnp.float32).reshape(BLOCK, KVH, group_size, HD)
        g_rows = lax.dynamic_slice_in_dim(upstream, block_id * BLOCK, BLOCK, 0).astype(jnp.float32).reshape(BLOCK, KVH, group_size, HD)
        named = refs[block_id]
        valid = named >= 0
        safe_ids = jnp.maximum(named, 0).astype(jnp.int32)
        key_rows = keys[safe_ids].astype(jnp.float32).reshape(MAXREF * IMG_TOK, KVH, HD)
        value_rows = values[safe_ids].astype(jnp.float32).reshape(MAXREF * IMG_TOK, KVH, HD)
        live_keys = jnp.repeat(valid, IMG_TOK)
        scores = jnp.einsum("tkgd,jkd->kgtj", q_rows, key_rows) * score_scale
        scores = jnp.where(live_keys, scores, jnp.float32(-1e30))
        highest = jnp.max(scores, axis=3, keepdims=True)
        log_total = highest + jnp.log(jnp.sum(jnp.exp(scores - highest), axis=3, keepdims=True))
        p_full = jnp.where(live_keys, jnp.exp(scores - log_total), jnp.float32(0.0))
        weights = lax.optimization_barrier(p_full.astype(jnp.bfloat16)).astype(jnp.float32)
        mixed_rows = jnp.einsum("kgtj,jkd->tkgd", weights, value_rows).reshape(BLOCK, HEADS * HD)
        attended = lax.optimization_barrier(mixed_rows.astype(jnp.bfloat16))
        attended_wide = attended.astype(jnp.float32).reshape(BLOCK, KVH, group_size, HD)
        deltas = jnp.einsum("tkgd,tkgd->kgt", g_rows, attended_wide)
        dweights = jnp.einsum("tkgd,jkd->kgtj", g_rows, value_rows)
        dscores = lax.optimization_barrier((p_full * (dweights - deltas[..., None])).astype(jnp.bfloat16)).astype(jnp.float32)
        q_grad = (jnp.einsum("kgtj,jkd->tkgd", dscores, key_rows) * score_scale).reshape(BLOCK, HEADS * HD).astype(jnp.bfloat16)
        keep = valid.astype(jnp.float32)[:, None, None]
        k_grad = (jnp.einsum("kgtj,tkgd->jkd", dscores, q_rows) * score_scale).reshape(MAXREF, IMG_TOK, key_width) * keep
        v_grad = jnp.einsum("kgtj,tkgd->jkd", weights, g_rows).reshape(MAXREF, IMG_TOK, key_width) * keep
        return attended, q_grad, k_grad, v_grad, safe_ids

    def block_step(running, block_id):
        attended, q_grad, k_grad, v_grad, safe_ids = block_terms(block_id)
        key_total = running[0].at[safe_ids].add(k_grad)
        value_total = running[1].at[safe_ids].add(v_grad)
        return (key_total, value_total), (attended, q_grad)

    zero_tiles = jnp.zeros((IMAGES, IMG_TOK, key_width), jnp.float32)
    totals, stacked = lax.scan(block_step, (zero_tiles, zero_tiles), jnp.arange(BLOCKS, dtype=jnp.int32))
    attended = stacked[0].reshape(TOKENS, HEADS * HD)
    query_grad = stacked[1].reshape(TOKENS, HEADS * HD)
    return (attended, query_grad, totals[0], totals[1])
```

```python
import functools

import jax
import jax.numpy as jnp
from jax import lax
from jax.experimental import pallas as pl
from jax.experimental.pallas import tpu as pltpu
from jax.sharding import PartitionSpec as P

HD = 128
BLOCK = 128
STEP = 2
TOK = 1601
TP = 1616
LP = 1664
NH = 8
EARLY = 5
LANES = 2 * BLOCK
CHUNKS = tuple((i * 256, 256) for i in range(6)) + ((1536, 80),)
SLABS = ((0, 816), (816, 800))
LOG2E = 1.4426950408889634
SCALE = HD**-0.5
LOW = -1e30
MESH = pl.DeviceIdType.MESH
OFFSETS = (-2, -1, 1, 2)
bf16 = jnp.bfloat16
f32 = jnp.float32


def mm(a, b):
    return lax.dot_general(a, b, (((1,), (0,)), ((), ())), preferred_element_type=f32)


def mm_nt(a, b):
    return lax.dot_general(a, b, (((1,), (1,)), ((), ())), preferred_element_type=f32)


def kernel(
    q_ref,
    k_ref,
    v_ref,
    refs_ref,
    g_ref,
    att_ref,
    qgrad_ref,
    dk,
    dv,
    qg,
    kp,
    vp,
    vt,
    kt,
    e_s,
    s_s,
    o_s,
    dq_s,
    m_s,
    w_s,
    st_own,
    st_rcv,
    snd,
    rcv,
    dk_prev,
    dv_prev,
    kv_snd,
    kv_rcv,
    msk,
    msk_rcv,
    live,
    q_send,
    q_recv,
    kv_send,
    kv_recv,
    back_send,
    back_recv,
    ret_send,
    ret_recv,
    st_send,
    st_recv,
    msk_send,
    msk_recv,
):
    n = lax.axis_size("ctx")
    me = lax.axis_index("ctx")

    def at(offset):
        return {"ctx": lax.rem(me + (n + offset), n)}

    def remote(src, dst, ssem, rsem, offset):
        return pltpu.make_async_remote_copy(
            src_ref=src,
            dst_ref=dst,
            send_sem=ssem,
            recv_sem=rsem,
            device_id=at(offset),
            device_id_type=MESH,
        )

    def q_copy(h):
        return remote(qg.at[0, h], qg.at[1, h], q_send.at[h], q_recv.at[h], -STEP)

    def kv_copy(i):
        ref = (kp, vp)[i]
        return remote(ref.at[0], ref.at[1], kv_send.at[i], kv_recv.at[i], 1)

    def back_copy(i):
        return remote(kv_snd.at[i], kv_rcv.at[i], back_send.at[i], back_recv.at[i], -1)

    def ret_copy(h, part):
        return remote(
            snd.at[part, h],
            rcv.at[part, h],
            ret_send.at[part, h],
            ret_recv.at[part, h],
            STEP,
        )

    def st_copy(h, block):
        other = 1 - block
        offset = -STEP if block == 0 else STEP
        return remote(
            st_own.at[block, h],
            st_rcv.at[other, h],
            st_send.at[block, h],
            st_recv.at[other, h],
            offset,
        )

    def st_arrival(h, block):
        return remote(
            st_own.at[block, h],
            st_rcv.at[block, h],
            st_send.at[block, h],
            st_recv.at[block, h],
            STEP,
        )

    def msk_copy():
        return remote(msk.at[1], msk_rcv, msk_send.at[0], msk_recv.at[0], -STEP)

    def head_cols(h):
        return pl.ds(pl.multiple_of(h * HD, HD), HD)

    def load_head(h):
        cols = head_cols(h)
        qg[0, h, 0:HD, :] = q_ref[:, cols].T
        qg[0, h, HD : 2 * HD, :] = g_ref[:, cols].T

    def wide(h, part):
        rows = slice(part * HD, (part + 1) * HD)
        return jnp.concatenate([qg[b, h, rows, :] for b in range(2)], 1)

    def turn(img, src, dst):
        for i in range(13):
            size = min(128, TP - i * 128)
            rows = pl.ds(i * 128, size)
            dst[img, 0:HD, rows] = src[img, rows, :].T

    barrier = pltpu.get_barrier_semaphore()
    for e in OFFSETS:
        pl.semaphore_signal(barrier, inc=1, device_id=at(e), device_id_type=MESH)
    for ref, src in ((kp, k_ref), (vp, v_ref)):
        ref[0, pl.ds(TP - 16, 16), :] = jnp.zeros((16, HD), bf16)
        ref[0, 0:TOK, :] = src[0]
    load_head(0)
    named = refs_ref[...]
    for d in range(4):
        hit = (named == me - d) & (me - d >= 0)
        hit = jnp.max(jnp.where(hit, 1.0, 0.0), axis=1, keepdims=True)
        msk[d // 2, d % 2] = jnp.broadcast_to(hit, (8, BLOCK))
    pl.semaphore_wait(barrier, len(OFFSETS))
    q_copy(0).start()
    kv_copy(0).start()
    msk_copy().start()
    kv_copy(1).start()

    def load_rest(h, carry):
        load_head(h)
        q_copy(h).start()
        return carry

    lax.fori_loop(1, NH, load_rest, 0)
    turn(0, vp, vt)
    turn(0, kp, kt)
    for img in range(2):
        vt[img, HD : HD + 16, :] = jnp.ones((16, LP), bf16)
    dk[...] = jnp.zeros_like(dk)
    dv[...] = jnp.zeros_like(dv)
    dk_prev[...] = jnp.zeros_like(dk_prev)
    dv_prev[...] = jnp.zeros_like(dv_prev)
    msk_copy().wait_recv()
    for img in range(2):
        live[img, :, 0:BLOCK] = msk[0, img]
        live[img, :, BLOCK:LANES] = msk_rcv[img]

    def scores(h):
        q_copy(h).wait_recv()
        scaled = wide(h, 0).astype(f32) * (LOG2E * SCALE)
        high = scaled.astype(bf16)
        low = (scaled - high.astype(f32)).astype(bf16)
        both = jnp.concatenate([high, low], 0)
        tops = []
        for img in range(2):
            m = jnp.full((8, LANES), LOW, f32)
            for first, size in CHUNKS:
                rows = pl.ds(first, size)
                k = kp[img, rows, :]
                s = mm(jnp.concatenate([k, k], 1), both)
                if first + size > TOK:
                    row = lax.broadcasted_iota(jnp.int32, (size, LANES), 0)
                    s = jnp.where(row < TOK - first, s, LOW)
                s_s[img, rows, :] = s
                m = jnp.maximum(m, jnp.max(s.reshape(size // 8, 8, LANES), 0))
            m = jnp.max(m, 0, keepdims=True)
            tops.append(jnp.where(live[img, 0:1, :] > 0.5, m, LOW))
        m = jnp.maximum(tops[0], tops[1])
        m_s[h] = m
        o = jnp.zeros((HD + 16, LANES), f32)
        for img in range(2):
            shift = jnp.where(live[img, 0:1, :] > 0.5, m, -LOW)
            for first, size in CHUNKS:
                rows = pl.ds(first, size)
                e = jnp.exp2(s_s[img, rows, :] - shift).astype(bf16)
                e_s[h, img, rows, :] = e
                if img == 0:
                    o = o + mm(vt[img, :, rows], e)
        o_s[h] = o

    def stats(h):
        o = o_s[h] + mm(vt[1, :, 0:TP], e_s[h, 1])
        o_s[h] = o
        total = o[HD : HD + 1]
        some = total > 0.0
        total = jnp.where(some, total, 1.0)
        grads = wide(h, 1).astype(f32)
        delta = jnp.sum(o[0:HD] * grads, axis=0, keepdims=True) / total
        lse = jnp.where(some, m_s[h] + jnp.log(total) * LOG2E, LOW)
        for b in range(2):
            at_b = slice(b * BLOCK, (b + 1) * BLOCK)
            st_own[b, h, 0:1, :] = lse[:, at_b]
            st_own[b, h, 1:2, :] = delta[:, at_b]
        for b in range(2):
            st_copy(h, b).start()

    def merge(h):
        sides = []
        for b in range(2):
            st_arrival(h, b).wait_recv()
        for ref in (st_own, st_rcv):
            lse = jnp.concatenate([ref[b, h, 0:1, :] for b in range(2)], 1)
            delta = jnp.concatenate([ref[b, h, 1:2, :] for b in range(2)], 1)
            sides.append((lse, delta))
        top = jnp.maximum(sides[0][0], sides[1][0])
        parts = [jnp.exp2(lse - top) for lse, delta in sides]
        inverse = 1.0 / (parts[0] + parts[1])
        delta = (parts[0] * sides[0][1] + parts[1] * sides[1][1]) * inverse
        weight = jnp.exp2(m_s[h] - top) * inverse
        w_s[h, 0:1, :] = weight
        w_s[h, 1:2, :] = delta
        o = o_s[h, 0:HD, :] * weight
        o_s[h, 0:HD, :] = o
        snd[0, h] = o[:, BLOCK:LANES].astype(bf16)
        ret_copy(h, 0).start()

    def backward(h, img, dk_to, dv_to):
        w = w_s[h, 0:1, :]
        delta = w_s[h, 1:2, :]
        q = wide(h, 0)
        g = wide(h, 1)
        gw = (g.astype(f32) * w).astype(bf16)
        qw = (q.astype(f32) * w).astype(bf16)
        dq = jnp.zeros((HD, LANES), f32)
        for first, size in SLABS:
            rows = pl.ds(first, size)
            kept = min(size, dk_to.shape[0] - first)
            e = e_s[h, img, rows, :]
            dp = mm(vp[img, rows, :], g)
            ds = (e.astype(f32) * (dp - delta)).astype(bf16)
            dq = dq + mm(kt[img, :, rows], ds)
            dv_to[pl.ds(first, kept), :] += mm_nt(e, gw)[0:kept]
            dk_to[pl.ds(first, kept), :] += mm_nt(ds, qw)[0:kept]
        dq = dq * (w * SCALE)
        if img == 1:
            dq_s[h] = dq
        else:
            dq = dq + dq_s[h]
            dq_s[h] = dq
            snd[1, h] = dq[:, BLOCK:LANES].astype(bf16)
            ret_copy(h, 1).start()

    def each(first, last, *steps):
        def body(h, carry):
            for step in steps:
                step(h)
            return carry

        lax.fori_loop(first, last, body, 0)

    kv_copy(0).wait_recv()
    turn(1, kp, kt)
    each(0, EARLY, scores)
    kv_copy(1).wait_recv()
    turn(1, vp, vt)
    each(0, EARLY, stats)
    each(EARLY, NH, scores, stats)
    each(0, NH, merge, lambda h: backward(h, 1, dk_prev, dv_prev))
    for i, ref in enumerate((dv_prev, dk_prev)):
        kv_snd[i] = ref[...].astype(bf16)
        back_copy(i).start()
    each(0, NH, lambda h: backward(h, 0, dk, dv))

    def finish(h):
        cols = head_cols(h)
        for part, (ref, out) in enumerate(((o_s, att_ref), (dq_s, qgrad_ref))):
            ret_copy(h, part).wait_recv()
            total = ref[h, 0:HD, 0:BLOCK] + rcv[part, h].astype(f32)
            out[:, cols] = total.T.astype(bf16)

    each(0, NH, finish)
    back_copy(0).wait_recv()
    dv[...] = dv[...] + kv_rcv[0, 0:TOK, :].astype(f32)
    back_copy(1).wait_recv()
    dk[...] = (dk[...] + kv_rcv[1, 0:TOK, :].astype(f32)) * SCALE

    def sent(h):
        q_copy(h).wait_send()
        for i in range(2):
            ret_copy(h, i).wait_send()
            st_copy(h, i).wait_send()

    each(0, NH, sent)
    for i in range(2):
        kv_copy(i).wait_send()
        back_copy(i).wait_send()
    msk_copy().wait_send()


def write_back(att, qgrad, dk, dv, att_out, qgrad_out, dk_out, dv_out, sems):
    copies = [
        pltpu.make_async_copy(dk, dk_out.at[:, 0, :], sems.at[0]),
        pltpu.make_async_copy(dv, dv_out.at[:, 0, :], sems.at[1]),
        pltpu.make_async_copy(att, att_out, sems.at[2]),
        pltpu.make_async_copy(qgrad, qgrad_out, sems.at[3]),
    ]
    for copy in copies:
        copy.start()
    for copy in copies:
        copy.wait()


def on_device(queries, keys, values, refs, upstream):
    vmem = pl.BlockSpec(memory_space=pltpu.VMEM)
    anywhere = pl.BlockSpec(memory_space=pl.ANY)
    dma = pltpu.SemaphoreType.DMA
    attended, query_grad, key_grad, value_grad = pl.pallas_call(
        kernel,
        out_shape=[
            pltpu.MemorySpace.VMEM(queries.shape, bf16),
            pltpu.MemorySpace.VMEM(queries.shape, bf16),
            pltpu.MemorySpace.VMEM((TOK, HD), f32),
            pltpu.MemorySpace.VMEM((TOK, HD), f32),
        ],
        in_specs=[vmem] * 5,
        out_specs=[vmem] * 4,
        scratch_shapes=[
            pltpu.VMEM((2, NH, 2 * HD, BLOCK), bf16),
            pltpu.VMEM((2, TP, HD), bf16),
            pltpu.VMEM((2, TP, HD), bf16),
            pltpu.VMEM((2, HD + 16, LP), bf16),
            pltpu.VMEM((2, HD, LP), bf16),
            pltpu.VMEM((NH, 2, TP, LANES), bf16),
            pltpu.VMEM((2, TP, LANES), f32),
            pltpu.VMEM((NH, HD + 16, LANES), f32),
            pltpu.VMEM((NH, HD, LANES), f32),
            pltpu.VMEM((NH, 1, LANES), f32),
            pltpu.VMEM((NH, 2, LANES), f32),
            pltpu.VMEM((2, NH, 2, BLOCK), f32),
            pltpu.VMEM((2, NH, 2, BLOCK), f32),
            pltpu.VMEM((2, NH, HD, BLOCK), bf16),
            pltpu.VMEM((2, NH, HD, BLOCK), bf16),
            pltpu.VMEM((TP, HD), f32),
            pltpu.VMEM((TP, HD), f32),
            pltpu.VMEM((2, TP, HD), bf16),
            pltpu.VMEM((2, TP, HD), bf16),
            pltpu.VMEM((2, 2, 8, BLOCK), f32),
            pltpu.VMEM((2, 8, BLOCK), f32),
            pltpu.VMEM((2, 8, LANES), f32),
            dma((NH,)),
            dma((NH,)),
            dma((2,)),
            dma((2,)),
            dma((2,)),
            dma((2,)),
            dma((2, NH)),
            dma((2, NH)),
            dma((2, NH)),
            dma((2, NH)),
            dma((1,)),
            dma((1,)),
        ],
        compiler_params=pltpu.CompilerParams(
            collective_id=0, has_side_effects=True, vmem_limit_bytes=44 * 2**20
        ),
    )(queries, keys, values, refs, upstream)
    attended, query_grad, key_grad, value_grad = pl.pallas_call(
        write_back,
        out_shape=[
            jax.ShapeDtypeStruct(queries.shape, bf16),
            jax.ShapeDtypeStruct(queries.shape, bf16),
            jax.ShapeDtypeStruct((TOK, 1, HD), f32),
            jax.ShapeDtypeStruct((TOK, 1, HD), f32),
        ],
        in_specs=[vmem] * 4,
        out_specs=[anywhere] * 4,
        scratch_shapes=[dma((4,))],
        compiler_params=pltpu.CompilerParams(vmem_limit_bytes=4 * 2**20),
    )(attended, query_grad, key_grad, value_grad)
    return (
        attended,
        query_grad,
        key_grad.reshape(keys.shape),
        value_grad.reshape(keys.shape),
    )


def solution(mesh):
    return jax.shard_map(
        on_device,
        mesh=mesh,
        in_specs=(
            P(("dp", "ctx"), "tp"),
            P(("dp", "ctx"), None, "tp"),
            P(("dp", "ctx"), None, "tp"),
            P(("dp", "ctx"), None),
            P(("dp", "ctx"), "tp"),
        ),
        out_specs=(
            P(("dp", "ctx"), "tp"),
            P(("dp", "ctx"), "tp"),
            P(("dp", "ctx"), None, "tp"),
            P(("dp", "ctx"), None, "tp"),
        ),
        check_vma=False,
    )
```

```python
import functools

import jax
import jax.numpy as jnp
from jax import lax
from jax.experimental import pallas as pl
from jax.experimental.pallas import tpu as pltpu
from jax.sharding import PartitionSpec as P

HD = 128
BLOCK = 128
STEP = 2
TOK = 1601
TP = 1616
LP = 1664
NH = 8
PAIRS = NH // 2
LANES = 4 * BLOCK
CHUNKS = tuple((i * 256, 256) for i in range(6)) + ((1536, 80),)
ORDER = ((0, 0), (0, 1), (1, 0), (1, 1))
LOG2E = 1.4426950408889634
SCALE = HD**-0.5
LOW = -1e30
MESH = pl.DeviceIdType.MESH
OFFSETS = (-2, -1, 1, 2)
bf16 = jnp.bfloat16
f32 = jnp.float32


def mm(a, b):
    return lax.dot_general(a, b, (((1,), (0,)), ((), ())), preferred_element_type=f32)


def mm_nt(a, b):
    return lax.dot_general(a, b, (((1,), (1,)), ((), ())), preferred_element_type=f32)


def kernel(
    q_ref,
    k_ref,
    v_ref,
    refs_ref,
    g_ref,
    att_ref,
    qgrad_ref,
    dk,
    dv,
    rows_in,
    tokens_in,
    refs_in,
    qg,
    kp,
    vp,
    vt,
    kt,
    e_s,
    s_s,
    o_s,
    dq_s,
    m_s,
    l_s,
    w_s,
    d_s,
    lse_own,
    lse_rcv,
    del_own,
    del_rcv,
    snd,
    rcv,
    dk_prev,
    dv_prev,
    kv_snd,
    kv_rcv,
    msk,
    msk_rcv,
    live,
    in_sem,
    q_send,
    q_recv,
    kv_send,
    kv_recv,
    back_send,
    back_recv,
    ret_send,
    ret_recv,
    lse_send,
    lse_recv,
    del_send,
    del_recv,
    msk_send,
    msk_recv,
):
    n = lax.axis_size("ctx")
    me = lax.axis_index("ctx")

    def at(offset):
        return {"ctx": lax.rem(me + (n + offset), n)}

    def remote(src, dst, ssem, rsem, offset):
        return pltpu.make_async_remote_copy(
            src_ref=src,
            dst_ref=dst,
            send_sem=ssem,
            recv_sem=rsem,
            device_id=at(offset),
            device_id_type=MESH,
        )

    def q_copy(p, part):
        heads = pl.ds(2 * p, 2)
        return remote(
            qg.at[0, part, heads],
            qg.at[1, part, heads],
            q_send.at[part, p],
            q_recv.at[part, p],
            -STEP,
        )

    def kv_copy(i):
        ref = (kp, vp)[i]
        return remote(ref.at[0], ref.at[1], kv_send.at[i], kv_recv.at[i], 1)

    def back_copy(i):
        return remote(kv_snd.at[i], kv_rcv.at[i], back_send.at[i], back_recv.at[i], -1)

    def ret_copy(p, part):
        return remote(
            snd.at[part, p],
            rcv.at[part, p],
            ret_send.at[part, p],
            ret_recv.at[part, p],
            STEP,
        )

    def swap(own, taken, ssem, rsem, p, block):
        return remote(
            own.at[block, p],
            taken.at[1 - block, p],
            ssem.at[block, p],
            rsem.at[1 - block, p],
            -STEP if block == 0 else STEP,
        )

    def swapped(own, taken, ssem, rsem, p, block):
        return remote(
            own.at[block, p],
            taken.at[block, p],
            ssem.at[block, p],
            rsem.at[block, p],
            STEP,
        )

    lse_refs = (lse_own, lse_rcv, lse_send, lse_recv)
    del_refs = (del_own, del_rcv, del_send, del_recv)

    def give(refs, p, row):
        for i, (j, b) in enumerate(ORDER):
            refs[0][b, p, j : j + 1, :] = row[:, i * BLOCK : (i + 1) * BLOCK]
        for b in range(2):
            swap(*refs, p, b).start()

    def take(refs, p):
        for b in range(2):
            swapped(*refs, p, b).wait_recv()
        return [
            jnp.concatenate([r[b, p, j : j + 1, :] for j, b in ORDER], 1)
            for r in refs[:2]
        ]

    def msk_copy():
        return remote(msk.at[1], msk_rcv, msk_send.at[0], msk_recv.at[0], -STEP)

    def each(first, last, *steps):
        def body(i, carry):
            for step in steps:
                step(i)
            return carry

        lax.fori_loop(first, last, body, 0)

    def head_cols(h):
        return pl.ds(pl.multiple_of(h * HD, HD), HD)

    def load_head(h, part):
        qg[0, part, h] = rows_in[part, :, head_cols(h)].T

    def wide(p, part):
        return jnp.concatenate([qg[b, part, 2 * p + j] for j, b in ORDER], 1)

    def turn(img, src, dst):
        for i in range(13):
            size = min(128, TP - i * 128)
            rows = pl.ds(i * 128, size)
            dst[img, :, rows] = src[img, rows, :].T

    loads = [
        pltpu.make_async_copy(q_ref, rows_in.at[0], in_sem.at[0]),
        pltpu.make_async_copy(k_ref.at[0], tokens_in.at[0], in_sem.at[1]),
        pltpu.make_async_copy(v_ref.at[0], tokens_in.at[1], in_sem.at[2]),
        pltpu.make_async_copy(refs_ref, refs_in, in_sem.at[3]),
        pltpu.make_async_copy(g_ref, rows_in.at[1], in_sem.at[4]),
    ]
    for load in loads:
        load.start()
    barrier = pltpu.get_barrier_semaphore()
    for e in OFFSETS:
        pl.semaphore_signal(barrier, inc=1, device_id=at(e), device_id_type=MESH)
    dk[...] = jnp.zeros_like(dk)
    dv[...] = jnp.zeros_like(dv)
    dk_prev[...] = jnp.zeros_like(dk_prev)
    dv_prev[...] = jnp.zeros_like(dv_prev)
    for load in loads:
        load.wait()
    for i, ref in enumerate((kp, vp)):
        ref[0, pl.ds(TP - 16, 16), :] = jnp.zeros((16, HD), bf16)
        ref[0, 0:TOK, :] = tokens_in[i]
    named = refs_in[...]
    for d in range(4):
        hit = (named == me - d) & (me - d >= 0)
        hit = jnp.max(jnp.where(hit, 1.0, 0.0), axis=1, keepdims=True)
        msk[d // 2, d % 2] = jnp.broadcast_to(hit, (8, BLOCK))
    for h in range(NH):
        load_head(h, 0)
    pl.semaphore_wait(barrier, len(OFFSETS))
    q_copy(0, 0).start()
    kv_copy(0).start()
    msk_copy().start()
    for p in range(1, PAIRS):
        q_copy(p, 0).start()
    kv_copy(1).start()
    for p in range(PAIRS):
        load_head(2 * p, 1)
        load_head(2 * p + 1, 1)
    turn(0, vp, vt)
    turn(0, kp, kt)
    msk_copy().wait_recv()
    for img in range(2):
        for i, (j, b) in enumerate(ORDER):
            src = msk[0, img] if b == 0 else msk_rcv[img]
            live[img, :, i * BLOCK : (i + 1) * BLOCK] = src

    def scores(p, img):
        scaled = wide(p, 0).astype(f32) * (LOG2E * SCALE)
        high = scaled.astype(bf16)
        low = (scaled - high.astype(f32)).astype(bf16)
        both = jnp.concatenate([high, low], 0)
        m = jnp.full((8, LANES), LOW, f32)
        for first, size in CHUNKS:
            rows = pl.ds(first, size)
            k = kp[img, rows, :]
            s = mm(jnp.concatenate([k, k], 1), both)
            if first + size > TOK:
                row = lax.broadcasted_iota(jnp.int32, (size, LANES), 0)
                s = jnp.where(row < TOK - first, s, LOW)
            s_s[rows, :] = s
            m = jnp.maximum(m, jnp.max(s.reshape(size // 8, 8, LANES), 0))
        m = jnp.max(m, 0, keepdims=True)
        total = jnp.zeros((8, LANES), f32)
        o = jnp.zeros((HD, LANES), f32)
        for first, size in CHUNKS:
            rows = pl.ds(first, size)
            e = jnp.exp2(s_s[rows, :] - m)
            total = total + jnp.sum(e.reshape(size // 8, 8, LANES), 0)
            e = e.astype(bf16)
            e_s[p, img, rows, :] = e
            if img == 0:
                o = o + mm(vt[img, :, rows], e)
        if img == 0:
            o_s[p] = o
        m_s[p, img] = jnp.where(live[img, 0:1, :] > 0.5, m, LOW)
        l_s[p, img] = jnp.sum(total, 0, keepdims=True)

    def scores_own(p):
        q_copy(p, 0).wait_recv()
        scores(p, 0)

        @pl.when(p == 1)
        def _():
            q_copy(0, 1).start()

    def scores_prev(p):
        scores(p, 1)
        m = [m_s[p, img] for img in range(2)]
        top = jnp.maximum(m[0], m[1])
        total = sum(l_s[p, img] * jnp.exp2(m[img] - top) for img in range(2))
        give(lse_refs, p, top + jnp.log(total) * LOG2E)

        @pl.when(p + 1 < PAIRS)
        def _():
            q_copy(p + 1, 1).start()

    def merge(p):
        lses = take(lse_refs, p)
        top = jnp.maximum(lses[0], lses[1])
        inverse = 1.0 / (jnp.exp2(lses[0] - top) + jnp.exp2(lses[1] - top))
        for img in range(2):
            w_s[p, img] = jnp.exp2(m_s[p, img] - top) * inverse

    def values_back(p, img, dv_to):
        kept = dv_to.shape[0]
        gw = (wide(p, 1).astype(f32) * w_s[p, img]).astype(bf16)
        dv_to[...] += mm_nt(e_s[p, img], gw)[0:kept]

    def values_prev(p):
        merge(p)
        q_copy(p, 1).wait_recv()
        values_back(p, 1, dv_prev)

    def send_parts(p, part, total):
        for j in range(2):
            low = (2 * j + 1) * BLOCK
            snd[part, p, j] = total[:, low : low + BLOCK].astype(bf16)
        ret_copy(p, part).start()

    def outputs(p):
        o = o_s[p] * w_s[p, 0] + mm(vt[1, :, 0:TP], e_s[p, 1]) * w_s[p, 1]
        o_s[p] = o
        give(del_refs, p, jnp.sum(o * wide(p, 1).astype(f32), axis=0, keepdims=True))

    def send_output(p):
        send_parts(p, 0, o_s[p])

    def backward(p, img, dk_to):
        w = w_s[p, img]
        delta = d_s[p]
        kept = dk_to.shape[0]
        qw = (wide(p, 0).astype(f32) * w).astype(bf16)
        dp = mm(vp[img], wide(p, 1))
        ds = (e_s[p, img].astype(f32) * (dp - delta)).astype(bf16)
        dk_to[...] += mm_nt(ds, qw)[0:kept]
        return mm(kt[img, :, 0:TP], ds) * (w * SCALE)

    def backward_prev(p):
        deltas = take(del_refs, p)
        d_s[p] = deltas[0] + deltas[1]
        dq_s[p] = backward(p, 1, dk_prev)

    def backward_own(p):
        dq = backward(p, 0, dk) + dq_s[p]
        dq_s[p] = dq
        send_parts(p, 1, dq)

    def values_own(p):
        values_back(p, 0, dv)

    def backward_next(p):
        backward_prev(p + 1)

    def send_back(i, ref):
        kv_snd[i] = ref[...].astype(bf16)
        back_copy(i).start()

    last = PAIRS - 1
    each(0, last, scores_own)
    kv_copy(0).wait_recv()
    each(0, last, scores_prev)
    scores_own(last)
    scores_prev(last)
    turn(1, kp, kt)
    values_prev(0)
    values_prev(1)
    kv_copy(1).wait_recv()
    turn(1, vp, vt)
    outputs(0)
    outputs(1)
    send_output(0)
    values_prev(2)
    outputs(2)
    send_output(1)
    backward_prev(0)
    values_prev(last)
    outputs(last)
    send_back(0, dv_prev)
    each(2, PAIRS, send_output)
    each(0, 2, backward_own, backward_next)
    backward_prev(last)
    send_back(1, dk_prev)
    each(2, PAIRS, backward_own)
    each(0, PAIRS, values_own)

    def finish(part):
        ref, out = ((o_s, att_ref), (dq_s, qgrad_ref))[part]

        def step(p):
            ret_copy(p, part).wait_recv()
            for j in range(2):
                total = ref[p, :, 2 * j * BLOCK : (2 * j + 1) * BLOCK]
                total = total + rcv[part, p, j].astype(f32)
                out[:, head_cols(2 * p + j)] = total.T.astype(bf16)

        return step

    each(0, PAIRS, finish(0))
    back_copy(0).wait_recv()
    dv[...] = dv[...] + kv_rcv[0, 0:TOK, :].astype(f32)
    each(0, PAIRS, finish(1))
    back_copy(1).wait_recv()
    dk[...] = (dk[...] + kv_rcv[1, 0:TOK, :].astype(f32)) * SCALE

    def sent(p):
        for i in range(2):
            q_copy(p, i).wait_send()
            ret_copy(p, i).wait_send()
            swap(*lse_refs, p, i).wait_send()
            swap(*del_refs, p, i).wait_send()

    each(0, PAIRS, sent)
    for i in range(2):
        kv_copy(i).wait_send()
        back_copy(i).wait_send()
    msk_copy().wait_send()


def write_back(att, qgrad, dk, dv, att_out, qgrad_out, dk_out, dv_out, sems):
    copies = [
        pltpu.make_async_copy(dk, dk_out.at[:, 0, :], sems.at[0]),
        pltpu.make_async_copy(dv, dv_out.at[:, 0, :], sems.at[1]),
        pltpu.make_async_copy(att, att_out, sems.at[2]),
        pltpu.make_async_copy(qgrad, qgrad_out, sems.at[3]),
    ]
    for copy in copies:
        copy.start()
    for copy in copies:
        copy.wait()


def on_device(queries, keys, values, refs, upstream):
    vmem = pl.BlockSpec(memory_space=pltpu.VMEM)
    anywhere = pl.BlockSpec(memory_space=pl.ANY)
    dma = pltpu.SemaphoreType.DMA
    hbm = pltpu.MemorySpace.HBM
    queries, keys, values, refs, upstream = (
        pltpu.with_memory_space_constraint(x, hbm)
        for x in (queries, keys, values, refs, upstream)
    )
    attended, query_grad, key_grad, value_grad = pl.pallas_call(
        kernel,
        out_shape=[
            pltpu.MemorySpace.VMEM(queries.shape, bf16),
            pltpu.MemorySpace.VMEM(queries.shape, bf16),
            pltpu.MemorySpace.VMEM((TOK, HD), f32),
            pltpu.MemorySpace.VMEM((TOK, HD), f32),
        ],
        in_specs=[pl.BlockSpec(memory_space=hbm)] * 5,
        out_specs=[vmem] * 4,
        scratch_shapes=[
            pltpu.VMEM((2, BLOCK, NH * HD), bf16),
            pltpu.VMEM((2, TOK, HD), bf16),
            pltpu.VMEM((1, 4), jnp.int32),
            pltpu.VMEM((2, 2, NH, HD, BLOCK), bf16),
            pltpu.VMEM((2, TP, HD), bf16),
            pltpu.VMEM((2, TP, HD), bf16),
            pltpu.VMEM((2, HD, LP), bf16),
            pltpu.VMEM((2, HD, LP), bf16),
            pltpu.VMEM((PAIRS, 2, TP, LANES), bf16),
            pltpu.VMEM((TP, LANES), f32),
            pltpu.VMEM((PAIRS, HD, LANES), f32),
            pltpu.VMEM((PAIRS, HD, LANES), f32),
            pltpu.VMEM((PAIRS, 2, 1, LANES), f32),
            pltpu.VMEM((PAIRS, 2, 1, LANES), f32),
            pltpu.VMEM((PAIRS, 2, 1, LANES), f32),
            pltpu.VMEM((PAIRS, 1, LANES), f32),
            pltpu.VMEM((2, PAIRS, 2, BLOCK), f32),
            pltpu.VMEM((2, PAIRS, 2, BLOCK), f32),
            pltpu.VMEM((2, PAIRS, 2, BLOCK), f32),
            pltpu.VMEM((2, PAIRS, 2, BLOCK), f32),
            pltpu.VMEM((2, PAIRS, 2, HD, BLOCK), bf16),
            pltpu.VMEM((2, PAIRS, 2, HD, BLOCK), bf16),
            pltpu.VMEM((TP, HD), f32),
            pltpu.VMEM((TP, HD), f32),
            pltpu.VMEM((2, TP, HD), bf16),
            pltpu.VMEM((2, TP, HD), bf16),
            pltpu.VMEM((2, 2, 8, BLOCK), f32),
            pltpu.VMEM((2, 8, BLOCK), f32),
            pltpu.VMEM((2, 8, LANES), f32),
            dma((5,)),
            dma((2, PAIRS)),
            dma((2, PAIRS)),
            dma((2,)),
            dma((2,)),
            dma((2,)),
            dma((2,)),
            dma((2, PAIRS)),
            dma((2, PAIRS)),
            dma((2, PAIRS)),
            dma((2, PAIRS)),
            dma((2, PAIRS)),
            dma((2, PAIRS)),
            dma((1,)),
            dma((1,)),
        ],
        compiler_params=pltpu.CompilerParams(
            collective_id=0, has_side_effects=True, vmem_limit_bytes=48 * 2**20
        ),
    )(queries, keys, values, refs, upstream)
    attended, query_grad, key_grad, value_grad = pl.pallas_call(
        write_back,
        out_shape=[
            jax.ShapeDtypeStruct(queries.shape, bf16),
            jax.ShapeDtypeStruct(queries.shape, bf16),
            jax.ShapeDtypeStruct((TOK, 1, HD), f32),
            jax.ShapeDtypeStruct((TOK, 1, HD), f32),
        ],
        in_specs=[vmem] * 4,
        out_specs=[anywhere] * 4,
        scratch_shapes=[dma((4,))],
        compiler_params=pltpu.CompilerParams(vmem_limit_bytes=4 * 2**20),
    )(attended, query_grad, key_grad, value_grad)
    return (
        attended,
        query_grad,
        key_grad.reshape(keys.shape),
        value_grad.reshape(keys.shape),
    )


def solution(mesh):
    return jax.shard_map(
        on_device,
        mesh=mesh,
        in_specs=(
            P(("dp", "ctx"), "tp"),
            P(("dp", "ctx"), None, "tp"),
            P(("dp", "ctx"), None, "tp"),
            P(("dp", "ctx"), None),
            P(("dp", "ctx"), "tp"),
        ),
        out_specs=(
            P(("dp", "ctx"), "tp"),
            P(("dp", "ctx"), "tp"),
            P(("dp", "ctx"), None, "tp"),
            P(("dp", "ctx"), None, "tp"),
        ),
        check_vma=False,
    )
```
